256 devices in a mesh: dp: 16 (over x_lo, y, core), ctx: 16 (over z, x_hi).
Axes of the slice: x: 4 (x_hi: 2, x_lo: 2; x = x_hi * 2 + x_lo), y: 4, z: 8, core: 2. Of those that a mesh axis runs over, the one named last changes fastest.
Arguments:
- tokens: bfloat16 [16, 3072, 5120], P('dp', 'ctx'), may hold values from -6 to 6
- queries: bfloat16 [16, 3072, 4096], P('dp', 'ctx'), may hold values from -400 to 400
- key_matrix: bfloat16 [5120, 512], P('dp'), may hold values from -0.078125 to 0.078125
- value_matrix: bfloat16 [5120, 512], P('dp'), may hold values from -0.078125 to 0.078125
- doc_lengths: int32 [16, 8], P('dp'), may hold values from 1 to 1536, 3072 in all within a row
- block_order: int32 [16, 16], P('dp'), may hold values from 0 to 15, each once within a row
Outputs:
- attended: bfloat16 [16, 3072, 4096], P('dp', 'ctx')
The draws below stay inside these ranges and needn't reach their ends.
Inputs may be any that keep to these rules, and one draw needn't show every extreme that they name: `doc_lengths`: each row sums to 3072, its largest entry is exactly 1536. `block_order`: each row is a permutation of the blocks.
All inputs are finite; a program needn't handle non-finite values.
Results may differ from the reference program's by a relative error of at most 0.012.
The reference program's roundings to bfloat16 on the way count: a program that leaves them out, or rounds other values in their place, can miss the bound.
Values may be sent and summed in bfloat16 or wider, within the bound.
No kernel may reach another device: no remote copies, remote signals or barrier semaphores. Data moves between devices by JAX's collectives and lax.ppermute only.
A program may use at most 192 MiB of HBM per device.

```python
import math
import jax
import jax.numpy as jnp
import numpy as np
from jax import lax

MODEL_WIDTH = 5120
QUERY_HEAD_COUNT = 32
KEY_VALUE_HEADS = 4
HEAD_SIZE = 128
TOK_DEV = 192
NDOCS = 8
SEQ = 3072
N_DP = 16
N_CTX = 16


def draw_queries(key, part):
    key = jax.random.fold_in(key, 11)
    base_key = jax.random.fold_in(key, 0)
    shape = (N_DP, SEQ, QUERY_HEAD_COUNT * HEAD_SIZE)
    base = jnp.clip(jax.random.normal(base_key, shape, jnp.float32), -4.0, 4.0)
    return base.astype(jnp.bfloat16)


def levels(own_key, shape, cuts, smallest, top_value):
    def one(dim, blocks):
        heights = jax.random.uniform(jax.random.fold_in(jax.random.fold_in(own_key, 6), dim), (blocks,), jnp.float32, smallest / len(cuts), top_value / len(cuts))
        return jnp.repeat(jnp.exp(heights), shape[dim] // blocks).reshape((-1,) + (1,) * (len(shape) - dim - 1))

    gain = one(*cuts[0])
    for cut in cuts[1:]:
        gain = gain * one(*cut)
    return gain


def length_profile(count, total, most, slope):
    loads = [(1 << 20) // math.isqrt(grade ** slope) + 1 for grade in range(2, count + 1)]
    surplus, counts = total - most - (count - 1), [1] * (count - 1)
    while surplus > 0:
        free = [i for i in range(count - 1) if counts[i] < most]
        mass, left = sum([loads[i] for i in free]), surplus
        for i in free:
            extra = min(most - counts[i], max(1, left * loads[i] // mass), surplus)
            counts[i] = counts[i] + extra
            surplus = surplus - extra
    return np.array([most] + counts)


def ragged(stream_key, number_of, total, most, lean):
    if number_of == 2:
        one = jax.random.randint(stream_key, (), max(1, total - most), min(most, total - 1) + 1)
        return jnp.stack([one, total - one])
    sizes = jnp.asarray(length_profile(number_of, total, most, lean), jnp.int32)
    twos = (number_of - 1) // 2
    giver, taker = sizes[1:1 + 2 * twos:2], sizes[2:2 + 2 * twos:2]
    slack = jnp.minimum(giver - 1, most - taker)
    shifted = jax.random.randint(jax.random.fold_in(stream_key, 1), (twos,), 0, 1 << 20) % (slack + 1)
    sizes = sizes.at[1:1 + 2 * twos:2].set(giver - shifted).at[2:2 + 2 * twos:2].set(taker + shifted)
    return sizes[jax.random.permutation(jax.random.fold_in(stream_key, 2), number_of)]


def normal_values(own_key, extent, width, reach, pieces=(), kind=jnp.bfloat16):
    array = width * jax.random.normal(own_key, extent, jnp.float32)
    if pieces:
        array = array * levels(own_key, extent, pieces, -0.22, 0.18)
    return jnp.clip(array, -reach, reach).astype(kind)


def setup_inputs(seed: int = 0) -> dict:
    seeds = jax.random.split(jax.random.key(seed), 7)
    return {
        "tokens": normal_values(seeds[0], (N_DP, SEQ, MODEL_WIDTH), 1.0, 6.0, ((0, 16), (1, 16))),
        "queries": draw_queries(jax.random.fold_in(seeds[6], 71), 0),
        "key_matrix": normal_values(seeds[2], (MODEL_WIDTH, KEY_VALUE_HEADS * HEAD_SIZE), MODEL_WIDTH ** -0.5, 0.078125, ((0, 16),)),
        "value_matrix": normal_values(seeds[3], (MODEL_WIDTH, KEY_VALUE_HEADS * HEAD_SIZE), MODEL_WIDTH ** -0.5, 0.078125, ((0, 16),)),
        "doc_lengths": jax.vmap(lambda own: ragged(own, NDOCS, SEQ, SEQ // 2, 2))(jax.random.split(seeds[4], N_DP)).reshape((N_DP, NDOCS)).astype(jnp.int32),
        "block_order": jax.vmap(lambda own: jax.random.permutation(own, N_CTX))(jax.random.split(seeds[5], N_DP)).reshape((N_DP, N_CTX)).astype(jnp.int32),
    }


def reference(tokens, queries, key_matrix, value_matrix, doc_lengths, block_order):
    query_groups = QUERY_HEAD_COUNT // KEY_VALUE_HEADS
    score_scale = 1.0 / (HEAD_SIZE ** 0.5)

    def one_pack(pack_args):
        hidden, query_rows, lengths, order_row = pack_args
        row_index = jnp.arange(SEQ, dtype=jnp.int32)
        position = order_row[row_index // TOK_DEV] * TOK_DEV + row_index % TOK_DEV
        doc_ends = jnp.cumsum(lengths)
        document = jnp.sum((doc_ends[None, :] <= position[:, None]).astype(jnp.int32), axis=1)
        keys = jnp.dot(hidden, key_matrix, preferred_element_type=jnp.float32).astype(jnp.bfloat16)
        values = jnp.dot(hidden, value_matrix, preferred_element_type=jnp.float32).astype(jnp.bfloat16)
        allowed = (document[:, None] == document[None, :]) & (position[None, :] <= position[:, None])

        def one_head(head_index):
            kv_index = head_index // query_groups
            query_head = lax.dynamic_slice_in_dim(query_rows, head_index * HEAD_SIZE, HEAD_SIZE, 1)
            key_head = lax.dynamic_slice_in_dim(keys, kv_index * HEAD_SIZE, HEAD_SIZE, 1)
            value_head = lax.dynamic_slice_in_dim(values, kv_index * HEAD_SIZE, HEAD_SIZE, 1)
            scores = jnp.dot(query_head, key_head.T, preferred_element_type=jnp.float32) * score_scale
            scores = jnp.where(allowed, scores, -1e30)
            row_max = jnp.max(scores, axis=1, keepdims=True)
            weights = jnp.where(allowed, jnp.exp(scores - row_max), 0.0)
            numerator = jnp.dot(weights.astype(jnp.bfloat16), value_head, preferred_element_type=jnp.float32)
            return numerator / jnp.sum(weights, axis=1, keepdims=True)

        per_head = lax.map(one_head, jnp.arange(QUERY_HEAD_COUNT, dtype=jnp.int32))
        return jnp.transpose(per_head, (1, 0, 2)).reshape(SEQ, QUERY_HEAD_COUNT * HEAD_SIZE).astype(jnp.bfloat16)

    return lax.map(one_pack, (tokens, queries, doc_lengths, block_order))
```

```python
import functools
import jax
import jax.numpy as jnp
from jax import lax
from jax.experimental import pallas as pl
from jax.experimental.pallas import tpu as pltpu
from jax.sharding import PartitionSpec as P

HEAD = 128
GROUPS = 8
ROWS = 192
KV_HEADS = 4
DOCS = 8
SLOTS = 16
TILE = 256
LONGEST = 1536
MAX_TILES = -(-(LONGEST + ROWS - 1) // TILE)
KEYS = MAX_TILES * TILE
HOPS = (0, 1, -1, 2, -2, 3, -3, 4)
BOTH = ("dp", "ctx")
LOG2E = 1.4426950408889634
NEG = -1e30


def pairs(move):
    out = []
    for dp in range(16):
        for ctx in range(16):
            x, y, core, z = (ctx % 2) * 2 + dp // 8, (dp // 2) % 4, dp % 2, ctx // 2
            x, y, z, core = move(x, y, z, core)
            x, y, z, core = x % 4, y % 4, z % 8, core % 2
            out.append((dp * 16 + ctx, ((x % 2) * 8 + y * 2 + core) * 16 + z * 2 + x // 2))
    return out


OTHER_CORE = pairs(lambda x, y, z, c: (x, y, z, c + 1))
Y_UP = pairs(lambda x, y, z, c: (x, y + 1, z, c))
Y_DOWN = pairs(lambda x, y, z, c: (x, y - 1, z, c))
X_UP = pairs(lambda x, y, z, c: (x + 1, y, z, c))
X_DOWN = pairs(lambda x, y, z, c: (x - 1, y, z, c))
X_FLIP = pairs(lambda x, y, z, c: (x + 1 - 2 * (x % 2), y, z, c))
X_FAR = pairs(lambda x, y, z, c: (x + 2, y, z, c))
X_FAR_OTHER = pairs(lambda x, y, z, c: (x + 2, y, z, c + 1))
Z_RINGS = [[z * 2 + hi for z in range(8)] for hi in range(2)]
Z_UP = pairs(lambda x, y, z, c: (x, y, z + 1, c))
Z_DOWN = pairs(lambda x, y, z, c: (x, y, z - 1, c))
Z_UP2 = pairs(lambda x, y, z, c: (x, y, z + 2, c))
Z_DOWN2 = pairs(lambda x, y, z, c: (x, y, z - 2, c))


def send(value, route):
    return lax.ppermute(value, BOTH, route)


def my_place():
    dp, ctx = lax.axis_index("dp"), lax.axis_index("ctx")
    return dp // 8, (dp // 2) % 4, dp % 2, ctx // 2, ctx % 2


def pair_kernel(keys, values, take_keys, take_values, first, second, sems):
    core = my_place()[2]
    here = pl.ds(pl.multiple_of(core * 320, 16), 320)
    there = pl.ds(pl.multiple_of(320 - core * 320, 16), 320)

    def fill(keep, take):
        copies = []
        for head in range(KV_HEADS):
            at = pl.ds(head * HEAD, HEAD)
            out, i = (first, second)[head % 2], head // 2
            copies.append(pltpu.make_async_copy(keep.at[:, at], out.at[i, here, :], sems.at[2 * head]))
            copies.append(pltpu.make_async_copy(take.at[:, at], out.at[i, there, :], sems.at[2 * head + 1]))
        for copy in copies:
            copy.start()
        for copy in copies:
            copy.wait()

    @pl.when(core == 0)
    def _():
        fill(keys, take_keys)

    @pl.when(core != 0)
    def _():
        fill(values, take_values)


def project_kernel(mine, theirs, *refs):
    parts, outs = refs[:10], (refs[10:12], refs[12:14])
    x_lo, y = my_place()[:2]
    places = ((0, 0), (0, 1), (0, 3), (1, 0), (1, 1), (1, 3), (0, 2), (1, 2))
    total = None
    for i, (across, along) in enumerate(places):
        chip = ((x_lo + across) % 2) * 4 + (y + along) % 4
        columns = pl.ds(pl.multiple_of(chip * 640, 128), 640)
        if i < 6:
            pair = parts[i][0], parts[i][1]
        else:
            pair = parts[2 * i - 6][...], parts[2 * i - 5][...]
        rows = jnp.concatenate([mine[:, columns], theirs[:, columns]], axis=0)
        part = jnp.dot(rows, jnp.concatenate(pair, axis=1), preferred_element_type=jnp.float32)
        total = part if total is None else total + part
    total = total.astype(jnp.bfloat16)
    low = my_place()[4] == 0
    for pack, (here, away) in enumerate(outs):
        rows = total[pack * ROWS : (pack + 1) * ROWS]
        here[...] = jnp.where(low, rows[:, :HEAD], rows[:, HEAD:])
        away[...] = jnp.where(low, rows[:, HEAD:], rows[:, :HEAD])


def stack_kernel(first, second, third, fourth, out):
    for i, part in enumerate((first, second, third, fourth)):
        out[i] = part[...]


def ask_kernel(queries, out, sem):
    hi = my_place()[4]
    at = pl.multiple_of((1 - hi) * 2 * GROUPS * HEAD, HEAD)
    copy = pltpu.make_async_copy(queries.at[0, :, pl.ds(at, 2 * GROUPS * HEAD)], out, sem)
    copy.start()
    copy.wait()


def attend_kernel(order, lengths, q, *refs, scale, chunk, far, first_head, heads):
    pieces, (out, kbuf, vbuf, kturn, bias) = refs[:-5], refs[-5:]
    core, my_z, my_hi = my_place()[2:]
    block = order[0, my_z * 2 + ((1 - my_hi) if far else my_hi)]
    q_first = chunk * GROUPS + first_head if far else (my_hi * 2 + chunk) * GROUPS
    first = block * ROWS
    end = first + ROWS

    starts = []
    begin = jnp.int32(0)
    for j in range(DOCS):
        starts.append(begin)
        begin = begin + lengths[0, j]
    lo = jnp.int32(0)
    for start in starts:
        lo = jnp.where(start <= first, jnp.maximum(lo, start), lo)
    low_block = lo // ROWS

    kbuf[...] = jnp.zeros_like(kbuf)
    vbuf[...] = jnp.zeros_like(vbuf)

    for step in range(8):
        for side in range(2):
            hi = (my_hi + side) % 2
            whole = len(pieces) == 1
            held = order[0, (step if whole else (my_z + 8 + HOPS[step]) % 8) * 2 + hi]

            @pl.when((held >= low_block) & (held <= block))
            def _():
                at = pl.ds(pl.multiple_of(KEYS - (block - held + 1) * ROWS, 16), ROWS)
                if whole:
                    source, base = pieces[0].at[step], 2 * side
                elif step < 7:
                    source, base = pieces[step], 2 * side
                else:
                    source, base = pieces[7 + side], 0
                kbuf[at, :] = source[base + core]
                vbuf[at, :] = source[base + 1 - core]

    kturn[...] = kbuf[...].T

    row_pos = first + lax.broadcasted_iota(jnp.int32, (ROWS, TILE), 0)
    row_lo = jnp.zeros((ROWS, TILE), jnp.int32)
    for start in starts:
        row_lo = jnp.where(start <= row_pos, jnp.maximum(row_lo, start), row_lo)
    lane = lax.broadcasted_iota(jnp.int32, (ROWS, TILE), 1)
    for t in range(MAX_TILES):
        key_pos = end - KEYS + t * TILE + lane
        bias[:, t * TILE : (t + 1) * TILE] = jnp.where((key_pos >= row_lo) & (key_pos <= row_pos), 0.0, NEG)

    for head in range(heads):
        rows = q[:, pl.ds(pl.multiple_of((q_first + head) * HEAD, HEAD), HEAD)]
        scores = []
        top = None
        for t in range(MAX_TILES):
            cols = slice(t * TILE, (t + 1) * TILE)
            s = jnp.dot(rows, kturn[:, cols], preferred_element_type=jnp.float32) + bias[:, cols]
            scores.append(s)
            most = jnp.maximum(s[:, :HEAD], s[:, HEAD:])
            top = most if top is None else jnp.maximum(top, most)
        top = jnp.max(top, axis=1, keepdims=True)
        total = acc = None
        for t, s in enumerate(scores):
            w = jnp.exp2((s - top) * (scale * LOG2E))
            part = w[:, :HEAD] + w[:, HEAD:]
            total = part if total is None else total + part
            part = jnp.dot(
                w.astype(jnp.bfloat16), vbuf[t * TILE : (t + 1) * TILE, :], preferred_element_type=jnp.float32
            )
            acc = part if acc is None else acc + part
        done = acc / jnp.sum(total, axis=1, keepdims=True)
        out[:, head * HEAD : (head + 1) * HEAD] = done.astype(jnp.bfloat16)


def finish_kernel(mine_a, mine_b, back_a, back_b0, back_b1, out):
    low = my_place()[4] == 0
    wide, half = GROUPS * HEAD, GROUPS * HEAD // 2

    def fill(mine, back):
        out[0, :, mine * wide : (mine + 1) * wide] = mine_a[...]
        out[0, :, (mine + 1) * wide : (mine + 2) * wide] = mine_b[...]
        out[0, :, back * wide : (back + 1) * wide] = back_a[...]
        out[0, :, (back + 1) * wide : (back + 1) * wide + half] = back_b0[...]
        out[0, :, (back + 1) * wide + half : (back + 2) * wide] = back_b1[...]

    @pl.when(low)
    def _():
        fill(0, 2)

    @pl.when(jnp.logical_not(low))
    def _():
        fill(2, 0)


VMEM = pl.BlockSpec(memory_space=pltpu.VMEM)
SMEM = pl.BlockSpec(memory_space=pltpu.SMEM)


def project(mine, theirs, parts):
    return pl.pallas_call(
        project_kernel,
        out_shape=(jax.ShapeDtypeStruct((ROWS, HEAD), jnp.bfloat16),) * 4,
        in_specs=[VMEM] * 12,
        out_specs=(VMEM,) * 4,
        compiler_params=pltpu.CompilerParams(vmem_limit_bytes=14 << 20),
        cost_estimate=pl.CostEstimate(flops=2 * 384 * 5120 * 256, bytes_accessed=7 << 20, transcendentals=0),
    )(mine, theirs, *parts)


def stack_up(*parts):
    return pl.pallas_call(
        stack_kernel,
        out_shape=jax.ShapeDtypeStruct((4, ROWS, HEAD), jnp.bfloat16),
        in_specs=[VMEM] * 4,
        out_specs=VMEM,
        compiler_params=pltpu.CompilerParams(vmem_limit_bytes=2 << 20),
    )(*parts)


def finish(*parts):
    return pl.pallas_call(
        finish_kernel,
        out_shape=jax.ShapeDtypeStruct((1, ROWS, 4 * GROUPS * HEAD), jnp.bfloat16),
        in_specs=[VMEM] * 5,
        out_specs=VMEM,
        compiler_params=pltpu.CompilerParams(vmem_limit_bytes=8 << 20),
    )(*parts)


def ask(queries):
    return pl.pallas_call(
        ask_kernel,
        out_shape=jax.ShapeDtypeStruct((ROWS, 2 * GROUPS * HEAD), jnp.bfloat16),
        in_specs=[pl.BlockSpec(memory_space=pl.ANY)],
        out_specs=VMEM,
        scratch_shapes=[pltpu.SemaphoreType.DMA],
        compiler_params=pltpu.CompilerParams(vmem_limit_bytes=8 << 20),
    )(queries)


def pair_up(keys, values, take_keys, take_values):
    return pl.pallas_call(
        pair_kernel,
        out_shape=(jax.ShapeDtypeStruct((2, 640, HEAD), keys.dtype),) * 2,
        in_specs=[pl.BlockSpec(memory_space=pl.ANY)] * 4,
        out_specs=(VMEM, VMEM),
        scratch_shapes=[pltpu.SemaphoreType.DMA((8,))],
        compiler_params=pltpu.CompilerParams(vmem_limit_bytes=4 << 20),
    )(keys, values, take_keys, take_values)


def attend(order, lengths, q, pieces, chunk, far, first_head=0, heads=GROUPS):
    return pl.pallas_call(
        functools.partial(
            attend_kernel, scale=1.0 / HEAD**0.5, chunk=chunk, far=far, first_head=first_head, heads=heads
        ),
        out_shape=jax.ShapeDtypeStruct((ROWS, heads * HEAD), jnp.bfloat16),
        in_specs=[SMEM, SMEM] + [VMEM] * (1 + len(pieces)),
        out_specs=VMEM,
        scratch_shapes=[
            pltpu.VMEM((KEYS, HEAD), jnp.bfloat16),
            pltpu.VMEM((KEYS, HEAD), jnp.bfloat16),
            pltpu.VMEM((HEAD, KEYS), jnp.bfloat16),
            pltpu.VMEM((ROWS, KEYS), jnp.float32),
        ],
        compiler_params=pltpu.CompilerParams(vmem_limit_bytes=14 << 20),
        cost_estimate=pl.CostEstimate(
            flops=16 * ROWS * heads * KEYS * HEAD, bytes_accessed=4 << 20, transcendentals=ROWS * heads * KEYS
        ),
    )(order, lengths, q, *pieces)


def after(value, *others):
    return lax.optimization_barrier((value, *others))[0]


def tie(values, *others):
    return lax.optimization_barrier((*values, *others))[: len(values)]


def ring(own, *earlier):
    up1, down1 = send(own, Z_DOWN), send(own, Z_UP)
    up2, down2 = send(up1, Z_DOWN), send(down1, Z_UP)
    up2, down2 = tie((up2, down2), *earlier)
    up3, down3 = send(up2, Z_DOWN), send(down2, Z_UP)
    last0, last1 = send(up2[:2], Z_DOWN2), send(down2[2:], Z_UP2)
    return (own, up1, down1, up2, down2, up3, down3, last0, last1)


def on_device(tokens, queries, key_matrix, value_matrix, doc_lengths, block_order):
    tokens, queries = tokens[0], queries[0]
    first, second = pair_up(
        key_matrix, value_matrix, send(key_matrix, OTHER_CORE), send(value_matrix, OTHER_CORE)
    )
    theirs = send(after(tokens, first), OTHER_CORE)

    up, down, flip = send(first, Y_DOWN), send(first, Y_UP), send(first, X_FLIP)
    up, down = tie((up, down), flip)
    far0, far1 = send(up[0], Y_DOWN), send(down[1], Y_UP)
    fup, fdown = send(up, X_DOWN), send(down, X_UP)
    far0 = after(far0, theirs)
    ffar0, ffar1 = send(far0, X_DOWN), send(far1, X_UP)
    parts_a = (first, up, down, flip, fup, fdown, far0, far1, ffar0, ffar1)

    second = after(second, far0, far1)
    up, down, flip = send(second, Y_DOWN), send(second, Y_UP), send(second, X_FLIP)
    up, down, flip = tie((up, down, flip), fup, fdown, ffar0, ffar1)
    parts_a = tie(parts_a, up, down, flip)
    far0, far1 = send(up[0], Y_DOWN), send(down[1], Y_UP)
    fup, fdown = send(flip, Y_DOWN), send(flip, Y_UP)
    ffar0, ffar1 = send(far0, X_DOWN), send(far1, X_UP)
    parts_b = (second, up, down, flip, fup, fdown, far0, far1, ffar0, ffar1)

    def swapped(parts, *earlier):
        here, away, other_here, other_away = project(tokens, theirs, parts)
        pieces = (here, send(other_here, OTHER_CORE), send(away, X_FAR), send(other_away, X_FAR_OTHER))
        return stack_up(*tie(pieces, *earlier))

    own_a = swapped(parts_a, far0, far1)
    kv_a = ring(own_a)
    own_b = swapped(tie(parts_b, *kv_a[1:3]), *kv_a[3:5])
    give = ask(after(queries, own_a)[None])
    q_far = send(after(give, own_b), X_FAR)
    kv_b = ring(own_b, *kv_a[5:], q_far)

    far_a = attend(block_order, doc_lengths, q_far, kv_a, 0, True)
    back_a = send(far_a, X_FAR)
    mine_a = attend(block_order, doc_lengths, queries, kv_a, 0, False)
    half = GROUPS // 2
    back_b = []
    for part in range(2):
        far_b = attend(block_order, doc_lengths, q_far, tie(kv_b, mine_a), 1, True, part * half, half)
        back_b.append(send(far_b, X_FAR))
    mine_b = attend(block_order, doc_lengths, queries, kv_b, 1, False)
    return finish(mine_a, mine_b, back_a, *back_b)


def solution(mesh):
    return jax.shard_map(
        on_device,
        mesh=mesh,
        in_specs=(
            P("dp", "ctx", None),
            P("dp", "ctx", None),
            P("dp", None),
            P("dp", None),
            P("dp", None),
            P("dp", None),
        ),
        out_specs=P("dp", "ctx", None),
        check_vma=False,
    )
```

```python
import functools
import jax
import jax.numpy as jnp
from jax import lax
from jax.experimental import pallas as pl
from jax.experimental.pallas import tpu as pltpu
from jax.sharding import PartitionSpec as P

HEAD = 128
GROUPS = 8
ROWS = 192
KV_HEADS = 4
DOCS = 8
SLOTS = 16
TILE = 256
LONGEST = 1536
MAX_TILES = -(-(LONGEST + ROWS - 1) // TILE)
KEYS = MAX_TILES * TILE
HOPS = (0, 1, -1, 2, -2, 3, -3, 4)
BOTH = ("dp", "ctx")
LOG2E = 1.4426950408889634
NEG = -1e30


def pairs(move):
    out = []
    for dp in range(16):
        for ctx in range(16):
            x, y, core, z = (ctx % 2) * 2 + dp // 8, (dp // 2) % 4, dp % 2, ctx // 2
            x, y, z, core = move(x, y, z, core)
            x, y, z, core = x % 4, y % 4, z % 8, core % 2
            out.append((dp * 16 + ctx, ((x % 2) * 8 + y * 2 + core) * 16 + z * 2 + x // 2))
    return out


OTHER_CORE = pairs(lambda x, y, z, c: (x, y, z, c + 1))
Y_UP = pairs(lambda x, y, z, c: (x, y + 1, z, c))
Y_DOWN = pairs(lambda x, y, z, c: (x, y - 1, z, c))
X_UP = pairs(lambda x, y, z, c: (x + 1, y, z, c))
X_DOWN = pairs(lambda x, y, z, c: (x - 1, y, z, c))
X_FLIP = pairs(lambda x, y, z, c: (x + 1 - 2 * (x % 2), y, z, c))
X_FAR = pairs(lambda x, y, z, c: (x + 2, y, z, c))
X_FAR_OTHER = pairs(lambda x, y, z, c: (x + 2, y, z, c + 1))
Z_RINGS = [[z * 2 + hi for z in range(8)] for hi in range(2)]
Z_UP = pairs(lambda x, y, z, c: (x, y, z + 1, c))
Z_DOWN = pairs(lambda x, y, z, c: (x, y, z - 1, c))
Z_UP2 = pairs(lambda x, y, z, c: (x, y, z + 2, c))
Z_DOWN2 = pairs(lambda x, y, z, c: (x, y, z - 2, c))


def send(value, route):
    return lax.ppermute(value, BOTH, route)


def my_place():
    dp, ctx = lax.axis_index("dp"), lax.axis_index("ctx")
    return dp // 8, (dp // 2) % 4, dp % 2, ctx // 2, ctx % 2


def half_kernel(keys, values, *refs, mine):
    first, second = refs[-2:]
    core = my_place()[2]
    row = core * 320 if mine else 320 - core * 320
    rows = pl.ds(pl.multiple_of(row, 16), 320)

    def fill(source):
        for head in range(KV_HEADS):
            (first, second)[head % 2][head // 2, rows, :] = source[:, head * HEAD : (head + 1) * HEAD]

    @pl.when(core == 0)
    def _():
        fill(keys)

    @pl.when(core != 0)
    def _():
        fill(values)


def project_kernel(mine, theirs, *refs):
    parts, outs = refs[:10], (refs[10:12], refs[12:14])
    x_lo, y = my_place()[:2]
    places = ((0, 0), (0, 1), (0, 3), (1, 0), (1, 1), (1, 3), (0, 2), (1, 2))
    total = None
    for i, (across, along) in enumerate(places):
        chip = ((x_lo + across) % 2) * 4 + (y + along) % 4
        columns = pl.ds(pl.multiple_of(chip * 640, 128), 640)
        if i < 6:
            pair = parts[i][0], parts[i][1]
        else:
            pair = parts[2 * i - 6][...], parts[2 * i - 5][...]
        rows = jnp.concatenate([mine[:, columns], theirs[:, columns]], axis=0)
        part = jnp.dot(rows, jnp.concatenate(pair, axis=1), preferred_element_type=jnp.float32)
        total = part if total is None else total + part
    total = total.astype(jnp.bfloat16)
    low = my_place()[4] == 0
    for pack, (here, away) in enumerate(outs):
        rows = total[pack * ROWS : (pack + 1) * ROWS]
        here[...] = jnp.where(low, rows[:, :HEAD], rows[:, HEAD:])
        away[...] = jnp.where(low, rows[:, HEAD:], rows[:, :HEAD])


def stack_kernel(first, second, third, fourth, out):
    for i, part in enumerate((first, second, third, fourth)):
        out[i] = part[...]


def ask_kernel(queries, out, sem):
    hi = my_place()[4]
    at = pl.multiple_of((1 - hi) * 2 * GROUPS * HEAD, HEAD)
    copy = pltpu.make_async_copy(queries.at[0, :, pl.ds(at, 2 * GROUPS * HEAD)], out, sem)
    copy.start()
    copy.wait()


def attend_kernel(order, lengths, q, *refs, scale, chunk, far, first_head, heads):
    pieces, (out, kbuf, vbuf, kturn, bias) = refs[:-5], refs[-5:]
    core, my_z, my_hi = my_place()[2:]
    block = order[0, my_z * 2 + ((1 - my_hi) if far else my_hi)]
    q_first = chunk * GROUPS + first_head if far else (my_hi * 2 + chunk) * GROUPS
    first = block * ROWS
    end = first + ROWS

    starts = []
    begin = jnp.int32(0)
    for j in range(DOCS):
        starts.append(begin)
        begin = begin + lengths[0, j]
    lo = jnp.int32(0)
    for start in starts:
        lo = jnp.where(start <= first, jnp.maximum(lo, start), lo)
    low_block = lo // ROWS

    kbuf[...] = jnp.zeros_like(kbuf)
    vbuf[:, :HEAD] = jnp.zeros((KEYS, HEAD), jnp.bfloat16)
    vbuf[:, HEAD:] = jnp.ones((KEYS, HEAD), jnp.bfloat16)

    for step in range(8):
        for side in range(2):
            hi = (my_hi + side) % 2
            whole = len(pieces) == 1
            held = order[0, (step if whole else (my_z + 8 + HOPS[step]) % 8) * 2 + hi]

            @pl.when((held >= low_block) & (held <= block))
            def _():
                at = pl.ds(pl.multiple_of(KEYS - (block - held + 1) * ROWS, 16), ROWS)
                if whole:
                    source, base = pieces[0].at[step], 2 * side
                elif step < 7:
                    source, base = pieces[step], 2 * side
                else:
                    source, base = pieces[7 + side], 0
                kbuf[at, :] = source[base + core]
                vbuf[at, :HEAD] = source[base + 1 - core]

    kturn[...] = kbuf[...].T

    row_pos = first + lax.broadcasted_iota(jnp.int32, (ROWS, TILE), 0)
    row_lo = jnp.zeros((ROWS, TILE), jnp.int32)
    for start in starts:
        row_lo = jnp.where(start <= row_pos, jnp.maximum(row_lo, start), row_lo)
    lane = lax.broadcasted_iota(jnp.int32, (ROWS, TILE), 1)
    for t in range(MAX_TILES):
        key_pos = end - KEYS + t * TILE + lane
        bias[:, t * TILE : (t + 1) * TILE] = jnp.where((key_pos >= row_lo) & (key_pos <= row_pos), 0.0, NEG)

    for head in range(heads):
        rows = q[:, pl.ds(pl.multiple_of((q_first + head) * HEAD, HEAD), HEAD)]
        scores = []
        top = None
        for t in range(MAX_TILES):
            cols = slice(t * TILE, (t + 1) * TILE)
            s = jnp.dot(rows, kturn[:, cols], preferred_element_type=jnp.float32) + bias[:, cols]
            scores.append(s)
            most = jnp.maximum(s[:, :HEAD], s[:, HEAD:])
            top = most if top is None else jnp.maximum(top, most)
        top = jnp.max(top, axis=1, keepdims=True)
        acc = None
        for t, s in enumerate(scores):
            w = jnp.exp2((s - top) * (scale * LOG2E))
            part = jnp.dot(
                w.astype(jnp.bfloat16), vbuf[t * TILE : (t + 1) * TILE, :], preferred_element_type=jnp.float32
            )
            acc = part if acc is None else acc + part
        done = acc[:, :HEAD] / acc[:, HEAD:]
        out[:, head * HEAD : (head + 1) * HEAD] = done.astype(jnp.bfloat16)


def finish_kernel(mine_a, mine_b, back_a, back_b0, back_b1, out):
    low = my_place()[4] == 0
    wide, half = GROUPS * HEAD, GROUPS * HEAD // 2

    def fill(mine, back):
        out[0, :, mine * wide : (mine + 1) * wide] = mine_a[...]
        out[0, :, (mine + 1) * wide : (mine + 2) * wide] = mine_b[...]
        out[0, :, back * wide : (back + 1) * wide] = back_a[...]
        out[0, :, (back + 1) * wide : (back + 1) * wide + half] = back_b0[...]
        out[0, :, (back + 1) * wide + half : (back + 2) * wide] = back_b1[...]

    @pl.when(low)
    def _():
        fill(0, 2)

    @pl.when(jnp.logical_not(low))
    def _():
        fill(2, 0)


VMEM = pl.BlockSpec(memory_space=pltpu.VMEM)
SMEM = pl.BlockSpec(memory_space=pltpu.SMEM)


def project(mine, theirs, parts):
    return pl.pallas_call(
        project_kernel,
        out_shape=(jax.ShapeDtypeStruct((ROWS, HEAD), jnp.bfloat16),) * 4,
        in_specs=[VMEM] * 12,
        out_specs=(VMEM,) * 4,
        compiler_params=pltpu.CompilerParams(vmem_limit_bytes=14 << 20),
        cost_estimate=pl.CostEstimate(flops=2 * 384 * 5120 * 256, bytes_accessed=7 << 20, transcendentals=0),
    )(mine, theirs, *parts)


def stack_up(*parts):
    return pl.pallas_call(
        stack_kernel,
        out_shape=jax.ShapeDtypeStruct((4, ROWS, HEAD), jnp.bfloat16),
        in_specs=[VMEM] * 4,
        out_specs=VMEM,
        compiler_params=pltpu.CompilerParams(vmem_limit_bytes=2 << 20),
    )(*parts)


def finish(*parts):
    return pl.pallas_call(
        finish_kernel,
        out_shape=jax.ShapeDtypeStruct((1, ROWS, 4 * GROUPS * HEAD), jnp.bfloat16),
        in_specs=[VMEM] * 5,
        out_specs=VMEM,
        compiler_params=pltpu.CompilerParams(vmem_limit_bytes=8 << 20),
    )(*parts)


def ask(queries):
    return pl.pallas_call(
        ask_kernel,
        out_shape=jax.ShapeDtypeStruct((ROWS, 2 * GROUPS * HEAD), jnp.bfloat16),
        in_specs=[pl.BlockSpec(memory_space=pl.ANY)],
        out_specs=VMEM,
        scratch_shapes=[pltpu.SemaphoreType.DMA],
        compiler_params=pltpu.CompilerParams(vmem_limit_bytes=8 << 20),
    )(queries)


def half_fill(keys, values, *filled):
    shape = jax.ShapeDtypeStruct((2, 640, HEAD), keys.dtype)
    return pl.pallas_call(
        functools.partial(half_kernel, mine=not filled),
        out_shape=(shape, shape),
        in_specs=[VMEM] * (2 + len(filled)),
        out_specs=(VMEM, VMEM),
        input_output_aliases={2: 0, 3: 1} if filled else {},
        compiler_params=pltpu.CompilerParams(vmem_limit_bytes=6 << 20),
    )(keys, values, *filled)


def attend(order, lengths, q, pieces, chunk, far, first_head=0, heads=GROUPS):
    return pl.pallas_call(
        functools.partial(
            attend_kernel, scale=1.0 / HEAD**0.5, chunk=chunk, far=far, first_head=first_head, heads=heads
        ),
        out_shape=jax.ShapeDtypeStruct((ROWS, heads * HEAD), jnp.bfloat16),
        in_specs=[SMEM, SMEM] + [VMEM] * (1 + len(pieces)),
        out_specs=VMEM,
        scratch_shapes=[
            pltpu.VMEM((KEYS, HEAD), jnp.bfloat16),
            pltpu.VMEM((KEYS, 2 * HEAD), jnp.bfloat16),
            pltpu.VMEM((HEAD, KEYS), jnp.bfloat16),
            pltpu.VMEM((ROWS, KEYS), jnp.float32),
        ],
        compiler_params=pltpu.CompilerParams(vmem_limit_bytes=14 << 20),
        cost_estimate=pl.CostEstimate(
            flops=16 * ROWS * heads * KEYS * HEAD, bytes_accessed=4 << 20, transcendentals=ROWS * heads * KEYS
        ),
    )(order, lengths, q, *pieces)


def after(value, *others):
    return lax.optimization_barrier((value, *others))[0]


def tie(values, *others):
    return lax.optimization_barrier((*values, *others))[: len(values)]


def ring(own, *earlier):
    up1, down1 = send(own, Z_DOWN), send(own, Z_UP)
    up2, down2 = send(up1, Z_DOWN), send(down1, Z_UP)
    up2, down2 = tie((up2, down2), *earlier)
    up3, down3 = send(up2, Z_DOWN), send(down2, Z_UP)
    last0, last1 = send(up2[:2], Z_DOWN2), send(down2[2:], Z_UP2)
    return (own, up1, down1, up2, down2, up3, down3, last0, last1)


def on_device(tokens, queries, key_matrix, value_matrix, doc_lengths, block_order):
    tokens, queries = tokens[0], queries[0]
    take_keys, take_values = send(key_matrix, OTHER_CORE), send(value_matrix, OTHER_CORE)
    first, second = half_fill(take_keys, take_values, *half_fill(key_matrix, value_matrix))
    theirs = send(after(tokens, first), OTHER_CORE)

    up, down, flip = send(first, Y_DOWN), send(first, Y_UP), send(first, X_FLIP)
    up, down = tie((up, down), flip)
    far0, far1 = send(up[0], Y_DOWN), send(down[1], Y_UP)
    fup, fdown = send(up, X_DOWN), send(down, X_UP)
    far0 = after(far0, theirs)
    ffar0, ffar1 = send(far0, X_DOWN), send(far1, X_UP)
    parts_a = (first, up, down, flip, fup, fdown, far0, far1, ffar0, ffar1)

    second = after(second, far0, far1)
    up, down, flip = send(second, Y_DOWN), send(second, Y_UP), send(second, X_FLIP)
    up, down, flip = tie((up, down, flip), fup, fdown, ffar0, ffar1)
    parts_a = tie(parts_a, up, down, flip)
    far0, far1 = send(up[0], Y_DOWN), send(down[1], Y_UP)
    fup, fdown = send(flip, Y_DOWN), send(flip, Y_UP)
    ffar0, ffar1 = send(far0, X_DOWN), send(far1, X_UP)
    parts_b = (second, up, down, flip, fup, fdown, far0, far1, ffar0, ffar1)

    def swapped(parts, *earlier):
        here, away, other_here, other_away = project(tokens, theirs, parts)
        pieces = (here, send(other_here, OTHER_CORE), send(away, X_FAR), send(other_away, X_FAR_OTHER))
        return stack_up(*tie(pieces, *earlier))

    own_a = swapped(parts_a, far0, far1)
    kv_a = ring(own_a)
    own_b = swapped(tie(parts_b, *kv_a[1:3]), *kv_a[3:5])
    give = ask(after(queries, own_a)[None])
    q_far = send(after(give, own_b), X_FAR)
    kv_b = ring(own_b, *kv_a[5:], q_far)

    far_a = attend(block_order, doc_lengths, q_far, kv_a, 0, True)
    back_a = send(far_a, X_FAR)
    mine_a = attend(block_order, doc_lengths, queries, kv_a, 0, False)
    half = GROUPS // 2
    back_b = []
    for part in range(2):
        far_b = attend(block_order, doc_lengths, q_far, tie(kv_b, mine_a), 1, True, part * half, half)
        back_b.append(send(far_b, X_FAR))
    mine_b = attend(block_order, doc_lengths, queries, kv_b, 1, False)
    return finish(mine_a, mine_b, back_a, *back_b)


def solution(mesh):
    return jax.shard_map(
        on_device,
        mesh=mesh,
        in_specs=(
            P("dp", "ctx", None),
            P("dp", "ctx", None),
            P("dp", None),
            P("dp", None),
            P("dp", None),
            P("dp", None),
        ),
        out_specs=P("dp", "ctx", None),
        check_vma=False,
    )
```

```python
import functools
import jax
import jax.numpy as jnp
from jax import lax
from jax.experimental import pallas as pl
from jax.experimental.pallas import tpu as pltpu
from jax.sharding import PartitionSpec as P

HEAD = 128
GROUPS = 8
ROWS = 192
KV_HEADS = 4
DOCS = 8
SLOTS = 16
TILE = 256
LONGEST = 1536
MAX_TILES = -(-(LONGEST + ROWS - 1) // TILE)
KEYS = MAX_TILES * TILE
HOPS = (0, 1, -1, 2, -2, 3, -3, 4)
BOTH = ("dp", "ctx")
LOG2E = 1.4426950408889634
NEG = -1e30


def pairs(move):
    out = []
    for dp in range(16):
        for ctx in range(16):
            x, y, core, z = (ctx % 2) * 2 + dp // 8, (dp // 2) % 4, dp % 2, ctx // 2
            x, y, z, core = move(x, y, z, core)
            x, y, z, core = x % 4, y % 4, z % 8, core % 2
            out.append((dp * 16 + ctx, ((x % 2) * 8 + y * 2 + core) * 16 + z * 2 + x // 2))
    return out


OTHER_CORE = pairs(lambda x, y, z, c: (x, y, z, c + 1))
Y_UP = pairs(lambda x, y, z, c: (x, y + 1, z, c))
Y_DOWN = pairs(lambda x, y, z, c: (x, y - 1, z, c))
X_UP = pairs(lambda x, y, z, c: (x + 1, y, z, c))
X_DOWN = pairs(lambda x, y, z, c: (x - 1, y, z, c))
X_FLIP = pairs(lambda x, y, z, c: (x + 1 - 2 * (x % 2), y, z, c))
X_FAR = pairs(lambda x, y, z, c: (x + 2, y, z, c))
X_FAR_OTHER = pairs(lambda x, y, z, c: (x + 2, y, z, c + 1))
Z_RINGS = [[z * 2 + hi for z in range(8)] for hi in range(2)]
Z_UP = pairs(lambda x, y, z, c: (x, y, z + 1, c))
Z_DOWN = pairs(lambda x, y, z, c: (x, y, z - 1, c))
Z_UP2 = pairs(lambda x, y, z, c: (x, y, z + 2, c))
Z_DOWN2 = pairs(lambda x, y, z, c: (x, y, z - 2, c))


def send(value, route):
    return lax.ppermute(value, BOTH, route)


def my_place():
    dp, ctx = lax.axis_index("dp"), lax.axis_index("ctx")
    return dp // 8, (dp // 2) % 4, dp % 2, ctx // 2, ctx % 2


def half_kernel(keys, values, *refs, mine):
    first, second = refs[-2:]
    core = my_place()[2]
    row = core * 320 if mine else 320 - core * 320
    rows = pl.ds(pl.multiple_of(row, 16), 320)

    def fill(source):
        for head in range(KV_HEADS):
            (first, second)[head % 2][head // 2, rows, :] = source[:, head * HEAD : (head + 1) * HEAD]

    @pl.when(core == 0)
    def _():
        fill(keys)

    @pl.when(core != 0)
    def _():
        fill(values)


def project_kernel(mine, theirs, *refs):
    parts, outs = refs[:10], (refs[10:12], refs[12:14])
    x_lo, y = my_place()[:2]
    places = ((0, 0), (0, 1), (0, 3), (1, 0), (1, 1), (1, 3), (0, 2), (1, 2))
    total = None
    for i, (across, along) in enumerate(places):
        chip = ((x_lo + across) % 2) * 4 + (y + along) % 4
        columns = pl.ds(pl.multiple_of(chip * 640, 128), 640)
        if i < 6:
            pair = parts[i][0], parts[i][1]
        else:
            pair = parts[2 * i - 6][...], parts[2 * i - 5][...]
        rows = jnp.concatenate([mine[:, columns], theirs[:, columns]], axis=0)
        part = jnp.dot(rows, jnp.concatenate(pair, axis=1), preferred_element_type=jnp.float32)
        total = part if total is None else total + part
    total = total.astype(jnp.bfloat16)
    low = my_place()[4] == 0
    for pack, (here, away) in enumerate(outs):
        rows = total[pack * ROWS : (pack + 1) * ROWS]
        here[...] = jnp.where(low, rows[:, :HEAD], rows[:, HEAD:])
        away[...] = jnp.where(low, rows[:, HEAD:], rows[:, :HEAD])


def stack_kernel(first, second, third, fourth, out):
    for i, part in enumerate((first, second, third, fourth)):
        out[i] = part[...]


def ask_kernel(queries, out, sem):
    hi = my_place()[4]
    at = pl.multiple_of((1 - hi) * 2 * GROUPS * HEAD, HEAD)
    copy = pltpu.make_async_copy(queries.at[0, :, pl.ds(at, 2 * GROUPS * HEAD)], out, sem)
    copy.start()
    copy.wait()


def attend_kernel(order, lengths, q, *refs, scale, chunk, far, first_head, heads):
    pieces, (out, kbuf, vbuf, kturn, bias) = refs[:-5], refs[-5:]
    core, my_z, my_hi = my_place()[2:]
    block = order[0, my_z * 2 + ((1 - my_hi) if far else my_hi)]
    q_first = chunk * GROUPS + first_head if far else (my_hi * 2 + chunk) * GROUPS
    first = block * ROWS
    end = first + ROWS

    starts = []
    begin = jnp.int32(0)
    for j in range(DOCS):
        starts.append(begin)
        begin = begin + lengths[0, j]
    lo = jnp.int32(0)
    for start in starts:
        lo = jnp.where(start <= first, jnp.maximum(lo, start), lo)
    low_block = lo // ROWS

    kbuf[...] = jnp.zeros_like(kbuf)
    vbuf[:, :HEAD] = jnp.zeros((KEYS, HEAD), jnp.bfloat16)
    vbuf[:, HEAD:] = jnp.ones((KEYS, HEAD), jnp.bfloat16)

    for step in range(8):
        for side in range(2):
            hi = (my_hi + side) % 2
            whole = len(pieces) == 1
            held = order[0, (step if whole else (my_z + 8 + HOPS[step]) % 8) * 2 + hi]

            @pl.when((held >= low_block) & (held <= block))
            def _():
                at = pl.ds(pl.multiple_of(KEYS - (block - held + 1) * ROWS, 16), ROWS)
                if whole:
                    source, base = pieces[0].at[step], 2 * side
                elif step < 7:
                    source, base = pieces[step], 2 * side
                else:
                    source, base = pieces[7 + side], 0
                kbuf[at, :] = source[base + core]
                vbuf[at, :HEAD] = source[base + 1 - core]

    kturn[...] = kbuf[...].T

    row_pos = first + lax.broadcasted_iota(jnp.int32, (ROWS, TILE), 0)
    row_lo = jnp.zeros((ROWS, TILE), jnp.int32)
    for start in starts:
        row_lo = jnp.where(start <= row_pos, jnp.maximum(row_lo, start), row_lo)
    lane = lax.broadcasted_iota(jnp.int32, (ROWS, TILE), 1)
    for t in range(MAX_TILES):
        key_pos = end - KEYS + t * TILE + lane
        bias[:, t * TILE : (t + 1) * TILE] = jnp.where((key_pos >= row_lo) & (key_pos <= row_pos), 0.0, NEG)

    for head in range(heads):
        rows = q[:, pl.ds(pl.multiple_of((q_first + head) * HEAD, HEAD), HEAD)]
        scores = []
        top = None
        for t in range(MAX_TILES):
            cols = slice(t * TILE, (t + 1) * TILE)
            s = jnp.dot(rows, kturn[:, cols], preferred_element_type=jnp.float32) + bias[:, cols]
            scores.append(s)
            most = jnp.maximum(s[:, :HEAD], s[:, HEAD:])
            top = most if top is None else jnp.maximum(top, most)
        top = jnp.max(top, axis=1, keepdims=True)
        acc = None
        for t, s in enumerate(scores):
            w = jnp.exp2((s - top) * (scale * LOG2E))
            part = jnp.dot(
                w.astype(jnp.bfloat16), vbuf[t * TILE : (t + 1) * TILE, :], preferred_element_type=jnp.float32
            )
            acc = part if acc is None else acc + part
        done = acc[:, :HEAD] / acc[:, HEAD:]
        out[:, head * HEAD : (head + 1) * HEAD] = done.astype(jnp.bfloat16)


def finish_kernel(mine_a, mine_b, back_a, back_b0, back_b1, out):
    low = my_place()[4] == 0
    wide, half = GROUPS * HEAD, GROUPS * HEAD // 2

    def fill(mine, back):
        out[0, :, mine * wide : (mine + 1) * wide] = mine_a[...]
        out[0, :, (mine + 1) * wide : (mine + 2) * wide] = mine_b[...]
        out[0, :, back * wide : (back + 1) * wide] = back_a[...]
        out[0, :, (back + 1) * wide : (back + 1) * wide + half] = back_b0[...]
        out[0, :, (back + 1) * wide + half : (back + 2) * wide] = back_b1[...]

    @pl.when(low)
    def _():
        fill(0, 2)

    @pl.when(jnp.logical_not(low))
    def _():
        fill(2, 0)


VMEM = pl.BlockSpec(memory_space=pltpu.VMEM)
SMEM = pl.BlockSpec(memory_space=pltpu.SMEM)


def project(mine, theirs, parts):
    return pl.pallas_call(
        project_kernel,
        out_shape=(jax.ShapeDtypeStruct((ROWS, HEAD), jnp.bfloat16),) * 4,
        in_specs=[VMEM] * 12,
        out_specs=(VMEM,) * 4,
        compiler_params=pltpu.CompilerParams(vmem_limit_bytes=14 << 20),
        cost_estimate=pl.CostEstimate(flops=2 * 384 * 5120 * 256, bytes_accessed=7 << 20, transcendentals=0),
    )(mine, theirs, *parts)


def stack_up(*parts):
    return pl.pallas_call(
        stack_kernel,
        out_shape=jax.ShapeDtypeStruct((4, ROWS, HEAD), jnp.bfloat16),
        in_specs=[VMEM] * 4,
        out_specs=VMEM,
        compiler_params=pltpu.CompilerParams(vmem_limit_bytes=2 << 20),
    )(*parts)


def finish(*parts):
    return pl.pallas_call(
        finish_kernel,
        out_shape=jax.ShapeDtypeStruct((1, ROWS, 4 * GROUPS * HEAD), jnp.bfloat16),
        in_specs=[VMEM] * 5,
        out_specs=VMEM,
        compiler_params=pltpu.CompilerParams(vmem_limit_bytes=8 << 20),
    )(*parts)


def ask(queries):
    return pl.pallas_call(
        ask_kernel,
        out_shape=jax.ShapeDtypeStruct((ROWS, 2 * GROUPS * HEAD), jnp.bfloat16),
        in_specs=[pl.BlockSpec(memory_space=pl.ANY)],
        out_specs=VMEM,
        scratch_shapes=[pltpu.SemaphoreType.DMA],
        compiler_params=pltpu.CompilerParams(vmem_limit_bytes=8 << 20),
    )(queries)


def half_fill(keys, values, *filled):
    shape = jax.ShapeDtypeStruct((2, 640, HEAD), keys.dtype)
    return pl.pallas_call(
        functools.partial(half_kernel, mine=not filled),
        out_shape=(shape, shape),
        in_specs=[VMEM] * (2 + len(filled)),
        out_specs=(VMEM, VMEM),
        input_output_aliases={2: 0, 3: 1} if filled else {},
        compiler_params=pltpu.CompilerParams(vmem_limit_bytes=6 << 20),
    )(keys, values, *filled)


def attend(order, lengths, q, pieces, chunk, far, first_head=0, heads=GROUPS):
    return pl.pallas_call(
        functools.partial(
            attend_kernel, scale=1.0 / HEAD**0.5, chunk=chunk, far=far, first_head=first_head, heads=heads
        ),
        out_shape=jax.ShapeDtypeStruct((ROWS, heads * HEAD), jnp.bfloat16),
        in_specs=[SMEM, SMEM] + [VMEM] * (1 + len(pieces)),
        out_specs=VMEM,
        scratch_shapes=[
            pltpu.VMEM((KEYS, HEAD), jnp.bfloat16),
            pltpu.VMEM((KEYS, 2 * HEAD), jnp.bfloat16),
            pltpu.VMEM((HEAD, KEYS), jnp.bfloat16),
            pltpu.VMEM((ROWS, KEYS), jnp.float32),
        ],
        compiler_params=pltpu.CompilerParams(vmem_limit_bytes=14 << 20),
        cost_estimate=pl.CostEstimate(
            flops=16 * ROWS * heads * KEYS * HEAD, bytes_accessed=4 << 20, transcendentals=ROWS * heads * KEYS
        ),
    )(order, lengths, q, *pieces)


def after(value, *others):
    return lax.optimization_barrier((value, *others))[0]


def tie(values, *others):
    return lax.optimization_barrier((*values, *others))[: len(values)]


def ring(own, *earlier):
    up1, down1 = send(own, Z_DOWN), send(own, Z_UP)
    up2, down2 = send(up1, Z_DOWN), send(down1, Z_UP)
    up2, down2 = tie((up2, down2), *earlier)
    up3, down3 = send(up2, Z_DOWN), send(down2, Z_UP)
    last0, last1 = send(up2[:2], Z_DOWN2), send(down2[2:], Z_UP2)
    return (own, up1, down1, up2, down2, up3, down3, last0, last1)


def on_device(tokens, queries, key_matrix, value_matrix, doc_lengths, block_order):
    tokens, queries = tokens[0], queries[0]
    take_keys, take_values = send(key_matrix, OTHER_CORE), send(value_matrix, OTHER_CORE)
    first, second = half_fill(take_keys, take_values, *half_fill(key_matrix, value_matrix))
    theirs = send(after(tokens, first), OTHER_CORE)

    up, down, flip = send(first, Y_DOWN), send(first, Y_UP), send(first, X_FLIP)
    up, down = tie((up, down), flip)
    far0, far1 = send(up[0], Y_DOWN), send(down[1], Y_UP)
    fup, fdown = send(up, X_DOWN), send(down, X_UP)
    far0, far1 = tie((far0, far1), theirs)
    ffar0, ffar1 = send(far0, X_DOWN), send(far1, X_UP)
    parts_a = (first, up, down, flip, fup, fdown, far0, far1, ffar0, ffar1)

    second = after(second, far0, far1)
    up, down, flip = send(second, Y_DOWN), send(second, Y_UP), send(second, X_FLIP)
    up, down, flip = tie((up, down, flip), fup, fdown, ffar0, ffar1)
    parts_a = tie(parts_a, up, down)
    far0, far1 = send(up[0], Y_DOWN), send(down[1], Y_UP)
    fup, fdown = send(flip, Y_DOWN), send(flip, Y_UP)
    ffar0, ffar1 = send(far0, X_DOWN), send(far1, X_UP)
    parts_b = (second, up, down, flip, fup, fdown, far0, far1, ffar0, ffar1)

    def swapped(parts, *earlier):
        here, away, other_here, other_away = project(tokens, theirs, parts)
        pieces = (here, send(other_here, OTHER_CORE), send(away, X_FAR), send(other_away, X_FAR_OTHER))
        return stack_up(*tie(pieces, *earlier))

    own_a = swapped(parts_a, far0, far1)
    kv_a = ring(own_a)
    own_b = swapped(tie(parts_b, *kv_a[1:3]), *kv_a[3:5])
    give = ask(after(queries, own_a)[None])
    q_far = send(after(give, own_b), X_FAR)
    kv_b = ring(own_b, *kv_a[5:], q_far)

    far_a = attend(block_order, doc_lengths, q_far, kv_a, 0, True)
    back_a = send(far_a, X_FAR)
    mine_a = attend(block_order, doc_lengths, queries, kv_a, 0, False)
    half = GROUPS // 2
    back_b = []
    for part in range(2):
        far_b = attend(block_order, doc_lengths, q_far, tie(kv_b, mine_a), 1, True, part * half, half)
        back_b.append(send(far_b, X_FAR))
    mine_b = attend(block_order, doc_lengths, queries, kv_b, 1, False)
    return finish(mine_a, mine_b, back_a, *back_b)


def solution(mesh):
    return jax.shard_map(
        on_device,
        mesh=mesh,
        in_specs=(
            P("dp", "ctx", None),
            P("dp", "ctx", None),
            P("dp", None),
            P("dp", None),
            P("dp", None),
            P("dp", None),
        ),
        out_specs=P("dp", "ctx", None),
        check_vma=False,
    )
```

```python
import functools
import jax
import jax.numpy as jnp
from jax import lax
from jax.experimental import pallas as pl
from jax.experimental.pallas import tpu as pltpu
from jax.sharding import PartitionSpec as P

HEAD = 128
GROUPS = 8
ROWS = 192
KV_HEADS = 4
DOCS = 8
SLOTS = 16
TILE = 256
LONGEST = 1536
MAX_TILES = -(-(LONGEST + ROWS - 1) // TILE)
KEYS = MAX_TILES * TILE
HOPS = (0, 1, -1, 2, -2, 3, -3, 4)
BOTH = ("dp", "ctx")
LOG2E = 1.4426950408889634
NEG = -1e30


def pairs(move):
    out = []
    for dp in range(16):
        for ctx in range(16):
            x, y, core, z = (ctx % 2) * 2 + dp // 8, (dp // 2) % 4, dp % 2, ctx // 2
            x, y, z, core = move(x, y, z, core)
            x, y, z, core = x % 4, y % 4, z % 8, core % 2
            out.append((dp * 16 + ctx, ((x % 2) * 8 + y * 2 + core) * 16 + z * 2 + x // 2))
    return out


OTHER_CORE = pairs(lambda x, y, z, c: (x, y, z, c + 1))
Y_UP = pairs(lambda x, y, z, c: (x, y + 1, z, c))
Y_DOWN = pairs(lambda x, y, z, c: (x, y - 1, z, c))
X_UP = pairs(lambda x, y, z, c: (x + 1, y, z, c))
X_DOWN = pairs(lambda x, y, z, c: (x - 1, y, z, c))
X_FLIP = pairs(lambda x, y, z, c: (x + 1 - 2 * (x % 2), y, z, c))
X_FAR = pairs(lambda x, y, z, c: (x + 2, y, z, c))
X_FAR_OTHER = pairs(lambda x, y, z, c: (x + 2, y, z, c + 1))
Z_RINGS = [[z * 2 + hi for z in range(8)] for hi in range(2)]
Z_UP = pairs(lambda x, y, z, c: (x, y, z + 1, c))
Z_DOWN = pairs(lambda x, y, z, c: (x, y, z - 1, c))
Z_UP2 = pairs(lambda x, y, z, c: (x, y, z + 2, c))
Z_DOWN2 = pairs(lambda x, y, z, c: (x, y, z - 2, c))


def send(value, route):
    return lax.ppermute(value, BOTH, route)


def my_place():
    dp, ctx = lax.axis_index("dp"), lax.axis_index("ctx")
    return dp // 8, (dp // 2) % 4, dp % 2, ctx // 2, ctx % 2


def half_kernel(keys, values, *refs, mine):
    first, second = refs[-2:]
    core = my_place()[2]
    row = core * 320 if mine else 320 - core * 320
    rows = pl.ds(pl.multiple_of(row, 16), 320)

    def fill(source):
        for head in range(KV_HEADS):
            (first, second)[head % 2][head // 2, rows, :] = source[:, head * HEAD : (head + 1) * HEAD]

    @pl.when(core == 0)
    def _():
        fill(keys)

    @pl.when(core != 0)
    def _():
        fill(values)


def project_kernel(mine, theirs, *refs):
    parts, outs = refs[:10], (refs[10:12], refs[12:14])
    x_lo, y = my_place()[:2]
    places = ((0, 0), (0, 1), (0, 3), (1, 0), (1, 1), (1, 3), (0, 2), (1, 2))
    total = None
    for i, (across, along) in enumerate(places):
        chip = ((x_lo + across) % 2) * 4 + (y + along) % 4
        columns = pl.ds(pl.multiple_of(chip * 640, 128), 640)
        if i < 6:
            pair = parts[i][0], parts[i][1]
        else:
            pair = parts[2 * i - 6][...], parts[2 * i - 5][...]
        rows = jnp.concatenate([mine[:, columns], theirs[:, columns]], axis=0)
        part = jnp.dot(rows, jnp.concatenate(pair, axis=1), preferred_element_type=jnp.float32)
        total = part if total is None else total + part
    total = total.astype(jnp.bfloat16)
    low = my_place()[4] == 0
    for pack, (here, away) in enumerate(outs):
        rows = total[pack * ROWS : (pack + 1) * ROWS]
        here[...] = jnp.where(low, rows[:, :HEAD], rows[:, HEAD:])
        away[...] = jnp.where(low, rows[:, HEAD:], rows[:, :HEAD])


def stack_kernel(first, second, third, fourth, out):
    for i, part in enumerate((first, second, third, fourth)):
        out[i] = part[...]


def ask_kernel(queries, out, sem):
    hi = my_place()[4]
    at = pl.multiple_of((1 - hi) * 2 * GROUPS * HEAD, HEAD)
    copy = pltpu.make_async_copy(queries.at[0, :, pl.ds(at, 2 * GROUPS * HEAD)], out, sem)
    copy.start()
    copy.wait()


def attend_kernel(order, lengths, q, *refs, scale, chunk, far, first_head, heads):
    pieces, (out, kbuf, vbuf, kturn, bias) = refs[:-5], refs[-5:]
    core, my_z, my_hi = my_place()[2:]
    block = order[0, my_z * 2 + ((1 - my_hi) if far else my_hi)]
    q_first = chunk * GROUPS + first_head if far else (my_hi * 2 + chunk) * GROUPS
    first = block * ROWS
    end = first + ROWS

    starts = []
    begin = jnp.int32(0)
    for j in range(DOCS):
        starts.append(begin)
        begin = begin + lengths[0, j]
    lo = jnp.int32(0)
    for start in starts:
        lo = jnp.where(start <= first, jnp.maximum(lo, start), lo)
    low_block = lo // ROWS

    kbuf[...] = jnp.zeros_like(kbuf)
    vbuf[:, :HEAD] = jnp.zeros((KEYS, HEAD), jnp.bfloat16)
    vbuf[:, HEAD:] = jnp.ones((KEYS, HEAD), jnp.bfloat16)

    for step in range(8):
        for side in range(2):
            hi = (my_hi + side) % 2
            whole = len(pieces) == 1
            held = order[0, (step if whole else (my_z + 8 + HOPS[step]) % 8) * 2 + hi]

            @pl.when((held >= low_block) & (held <= block))
            def _():
                at = pl.ds(pl.multiple_of(KEYS - (block - held + 1) * ROWS, 16), ROWS)
                if whole:
                    source, base = pieces[0].at[step], 2 * side
                elif step < 7:
                    source, base = pieces[step], 2 * side
                else:
                    source, base = pieces[7 + side], 0
                kbuf[at, :] = source[base + core]
                vbuf[at, :HEAD] = source[base + 1 - core]

    kturn[...] = kbuf[...].T

    row_pos = first + lax.broadcasted_iota(jnp.int32, (ROWS, TILE), 0)
    row_lo = jnp.zeros((ROWS, TILE), jnp.int32)
    for start in starts:
        row_lo = jnp.where(start <= row_pos, jnp.maximum(row_lo, start), row_lo)
    lane = lax.broadcasted_iota(jnp.int32, (ROWS, TILE), 1)
    for t in range(MAX_TILES):
        key_pos = end - KEYS + t * TILE + lane
        bias[:, t * TILE : (t + 1) * TILE] = jnp.where((key_pos >= row_lo) & (key_pos <= row_pos), 0.0, NEG)

    for head in range(heads):
        rows = q[:, pl.ds(pl.multiple_of((q_first + head) * HEAD, HEAD), HEAD)]
        scores = []
        top = None
        for t in range(MAX_TILES):
            cols = slice(t * TILE, (t + 1) * TILE)
            s = jnp.dot(rows, kturn[:, cols], preferred_element_type=jnp.float32) + bias[:, cols]
            scores.append(s)
            most = jnp.maximum(s[:, :HEAD], s[:, HEAD:])
            top = most if top is None else jnp.maximum(top, most)
        top = jnp.max(top, axis=1, keepdims=True)
        acc = None
        for t, s in enumerate(scores):
            w = jnp.exp2((s - top) * (scale * LOG2E))
            part = jnp.dot(
                w.astype(jnp.bfloat16), vbuf[t * TILE : (t + 1) * TILE, :], preferred_element_type=jnp.float32
            )
            acc = part if acc is None else acc + part
        done = acc[:, :HEAD] / acc[:, HEAD:]
        out[:, head * HEAD : (head + 1) * HEAD] = done.astype(jnp.bfloat16)


def finish_kernel(*refs, first):
    count = 3 if first else 1
    parts, out, sems = refs[:count], refs[-2], refs[-1]
    hi = my_place()[4]
    wide = GROUPS * HEAD
    mine, back = hi * 2 * wide, (1 - hi) * 2 * wide
    spots = (mine, mine + wide, back) if first else (back + wide,)
    copies = []
    for i, (part, spot) in enumerate(zip(parts, spots)):
        at = pl.ds(pl.multiple_of(spot, HEAD), wide)
        copies.append(pltpu.make_async_copy(part, out.at[0, :, at], sems.at[i]))
    for copy in copies:
        copy.start()
    for copy in copies:
        copy.wait()


VMEM = pl.BlockSpec(memory_space=pltpu.VMEM)
SMEM = pl.BlockSpec(memory_space=pltpu.SMEM)


def project(mine, theirs, parts):
    return pl.pallas_call(
        project_kernel,
        out_shape=(jax.ShapeDtypeStruct((ROWS, HEAD), jnp.bfloat16),) * 4,
        in_specs=[VMEM] * 12,
        out_specs=(VMEM,) * 4,
        compiler_params=pltpu.CompilerParams(vmem_limit_bytes=14 << 20),
        cost_estimate=pl.CostEstimate(flops=2 * 384 * 5120 * 256, bytes_accessed=7 << 20, transcendentals=0),
    )(mine, theirs, *parts)


def stack_up(*parts):
    return pl.pallas_call(
        stack_kernel,
        out_shape=jax.ShapeDtypeStruct((4, ROWS, HEAD), jnp.bfloat16),
        in_specs=[VMEM] * 4,
        out_specs=VMEM,
        compiler_params=pltpu.CompilerParams(vmem_limit_bytes=2 << 20),
    )(*parts)


def finish(*parts, whole=None):
    place = pl.BlockSpec(memory_space=pl.ANY)
    extra = () if whole is None else (whole,)
    return pl.pallas_call(
        functools.partial(finish_kernel, first=whole is None),
        out_shape=jax.ShapeDtypeStruct((1, ROWS, 4 * GROUPS * HEAD), jnp.bfloat16),
        in_specs=[VMEM] * len(parts) + [place] * len(extra),
        out_specs=place,
        scratch_shapes=[pltpu.SemaphoreType.DMA((3,))],
        input_output_aliases={len(parts): 0} if extra else {},
        compiler_params=pltpu.CompilerParams(vmem_limit_bytes=4 << 20),
    )(*parts, *extra)


def ask(queries):
    return pl.pallas_call(
        ask_kernel,
        out_shape=jax.ShapeDtypeStruct((ROWS, 2 * GROUPS * HEAD), jnp.bfloat16),
        in_specs=[pl.BlockSpec(memory_space=pl.ANY)],
        out_specs=VMEM,
        scratch_shapes=[pltpu.SemaphoreType.DMA],
        compiler_params=pltpu.CompilerParams(vmem_limit_bytes=8 << 20),
    )(queries)


def half_fill(keys, values, *filled):
    shape = jax.ShapeDtypeStruct((2, 640, HEAD), keys.dtype)
    return pl.pallas_call(
        functools.partial(half_kernel, mine=not filled),
        out_shape=(shape, shape),
        in_specs=[VMEM] * (2 + len(filled)),
        out_specs=(VMEM, VMEM),
        input_output_aliases={2: 0, 3: 1} if filled else {},
        compiler_params=pltpu.CompilerParams(vmem_limit_bytes=6 << 20),
    )(keys, values, *filled)


def attend(order, lengths, q, pieces, chunk, far, first_head=0, heads=GROUPS):
    return pl.pallas_call(
        functools.partial(
            attend_kernel, scale=1.0 / HEAD**0.5, chunk=chunk, far=far, first_head=first_head, heads=heads
        ),
        out_shape=jax.ShapeDtypeStruct((ROWS, heads * HEAD), jnp.bfloat16),
        in_specs=[SMEM, SMEM] + [VMEM] * (1 + len(pieces)),
        out_specs=VMEM,
        scratch_shapes=[
            pltpu.VMEM((KEYS, HEAD), jnp.bfloat16),
            pltpu.VMEM((KEYS, 2 * HEAD), jnp.bfloat16),
            pltpu.VMEM((HEAD, KEYS), jnp.bfloat16),
            pltpu.VMEM((ROWS, KEYS), jnp.float32),
        ],
        compiler_params=pltpu.CompilerParams(vmem_limit_bytes=14 << 20),
        cost_estimate=pl.CostEstimate(
            flops=16 * ROWS * heads * KEYS * HEAD, bytes_accessed=4 << 20, transcendentals=ROWS * heads * KEYS
        ),
    )(order, lengths, q, *pieces)


def after(value, *others):
    return lax.optimization_barrier((value, *others))[0]


def tie(values, *others):
    return lax.optimization_barrier((*values, *others))[: len(values)]


def ring(own, *earlier):
    up1, down1 = send(own, Z_DOWN), send(own, Z_UP)
    up2, down2 = send(up1, Z_DOWN), send(down1, Z_UP)
    up2, down2 = tie((up2, down2), *earlier)
    up3, down3 = send(up2, Z_DOWN), send(down2, Z_UP)
    last0, last1 = send(up2[:2], Z_DOWN2), send(down2[2:], Z_UP2)
    return (own, up1, down1, up2, down2, up3, down3, last0, last1)


def on_device(tokens, queries, key_matrix, value_matrix, doc_lengths, block_order):
    tokens, queries = tokens[0], queries[0]
    take_keys, take_values = send(key_matrix, OTHER_CORE), send(value_matrix, OTHER_CORE)
    first, second = half_fill(take_keys, take_values, *half_fill(key_matrix, value_matrix))
    theirs = send(after(tokens, first), OTHER_CORE)

    up, down, flip = send(first, Y_DOWN), send(first, Y_UP), send(first, X_FLIP)
    up, down = tie((up, down), flip)
    far0, far1 = send(up[0], Y_DOWN), send(down[1], Y_UP)
    fup, fdown = send(up, X_DOWN), send(down, X_UP)
    far0, far1 = tie((far0, far1), theirs)
    ffar0, ffar1 = send(far0, X_DOWN), send(far1, X_UP)
    parts_a = (first, up, down, flip, fup, fdown, far0, far1, ffar0, ffar1)

    second = after(second, far0, far1)
    up, down, flip = send(second, Y_DOWN), send(second, Y_UP), send(second, X_FLIP)
    up, down, flip = tie((up, down, flip), fup, fdown, ffar0, ffar1)
    parts_a = tie(parts_a, up, down)
    far0, far1 = send(up[0], Y_DOWN), send(down[1], Y_UP)
    fup, fdown = send(flip, Y_DOWN), send(flip, Y_UP)
    ffar0, ffar1 = send(far0, X_DOWN), send(far1, X_UP)
    parts_b = (second, up, down, flip, fup, fdown, far0, far1, ffar0, ffar1)

    def swapped(parts, *earlier):
        here, away, other_here, other_away = project(tokens, theirs, parts)
        pieces = (here, send(other_here, OTHER_CORE), send(away, X_FAR), send(other_away, X_FAR_OTHER))
        return stack_up(*tie(pieces, *earlier))

    own_a = swapped(parts_a, far0, far1)
    kv_a = ring(own_a)
    own_b = swapped(tie(parts_b, *kv_a[1:3]), *kv_a[3:5])
    give = ask(after(queries, own_a)[None])
    q_far = send(after(give, own_b), X_FAR)
    kv_b = ring(own_b, *kv_a[5:], q_far)

    far_a = attend(block_order, doc_lengths, q_far, kv_a, 0, True)
    back_a = send(far_a, X_FAR)
    mine_a = attend(block_order, doc_lengths, queries, kv_a, 0, False)
    far_b = attend(block_order, doc_lengths, q_far, tie(kv_b, mine_a), 1, True)
    back_b = send(far_b, X_FAR)
    mine_b = attend(block_order, doc_lengths, queries, kv_b, 1, False)
    return finish(back_b, whole=finish(mine_a, mine_b, back_a))


def solution(mesh):
    return jax.shard_map(
        on_device,
        mesh=mesh,
        in_specs=(
            P("dp", "ctx", None),
            P("dp", "ctx", None),
            P("dp", None),
            P("dp", None),
            P("dp", None),
            P("dp", None),
        ),
        out_specs=P("dp", "ctx", None),
        check_vma=False,
    )
```
